256 devices in a mesh: row: 4 (over y_hi, core), col: 8 (over z), aux: 8 (over x, y_lo).
Axes of the slice: x: 4, y: 4 (y_hi: 2, y_lo: 2; y = y_hi * 2 + y_lo), z: 8, core: 2. Of those that a mesh axis runs over, the one named last changes fastest.
Arguments:
- integrals: bfloat16 [8, 256, 64, 3072], P('aux', ('row', 'col')), may hold values from -0.75 to 0.75
- block_mask: int32 [8, 64, 64], P('aux', ('row', 'col')), may hold values from 0 to 1, as said below
- block_slots: int32 [8, 64, 64], P('aux', ('row', 'col')), may hold values from -1 to 7, as said below
- orbitals: bfloat16 [64, 4096], replicated, may hold values from -0.107910156 to 0.107910156
Outputs:
- exchange_matrix: float32 [4096, 4, 1024], P(('row', 'aux'), None, 'col')
The draws below stay inside these ranges and needn't reach their ends.
Inputs may be any that keep to these rules, and one draw needn't show every extreme that they name: `block_mask`: within one device's tile (one auxiliary batch, the mu blocks of one row and col index pair, all lambda blocks) between 1 and 8 blocks survive, and in some tile exactly 8. `block_slots`: the surviving blocks of a tile are numbered 0, 1, 2, ... in row-major order of (mu block, lambda block); blocks that did not survive hold -1, and packed slots past a tile's count hold data that is never read.
All inputs are finite; a program needn't handle non-finite values.
Results may differ from the reference program's by a relative error of at most 0.0017.
Values may be sent and summed in bfloat16 or wider, within the bound.
No kernel may reach another device: no remote copies, remote signals or barrier semaphores. Data moves between devices by JAX's collectives and lax.ppermute only.
A program may use at most 128 MiB of HBM per device.

```python
import jax
import jax.numpy as jnp
from jax import lax

NBAS = 4096
BLK = 64
NOCC = 64
QDEV = 48
CAP = 8
NMB = 64
MB_DEV = 2
N_ROW = 4
N_COL = 8
N_AUX = 8


def screened_layout(key):
    tiles = N_AUX * N_ROW * N_COL
    positions = NMB // (N_ROW * N_COL) * NMB
    count_key, pick_key, order_key = jax.random.split(key, 3)
    counts = jax.random.randint(count_key, (tiles,), 1, CAP + 1)
    busiest = jax.random.randint(pick_key, (), 0, tiles)
    counts = jnp.where(jnp.arange(tiles) == busiest, CAP, counts)

    def ranking(tile_key):
        return jax.random.permutation(tile_key, positions)
    ranks = jax.vmap(ranking)(jax.random.split(order_key, tiles))
    present = (ranks < counts[:, None]).astype(jnp.int32)
    before = jnp.cumsum(present, axis=1) - present
    slots = jnp.where(present == 1, before, -1).astype(jnp.int32)
    return (present.reshape(N_AUX, NMB, NMB), slots.reshape(N_AUX, NMB, NMB))


def draw_block_mask(key, part):
    present, slots = screened_layout(key)
    return present


def draw_block_slots(key, part):
    present, slots = screened_layout(key)
    return slots


def steps_of(rng, shape, shards, low, top_value):
    factor_of, own = 1.0, jax.random.fold_in(rng, 6)
    for axis_at, shards_of in shards:
        heights = jnp.exp(jax.random.uniform(jax.random.fold_in(own, axis_at), (shards_of,), jnp.float32, low / len(shards), top_value / len(shards)))
        factor_of = factor_of * jnp.repeat(heights, shape[axis_at] // shards_of).reshape([-1 if axis == axis_at else 1 for axis in range(len(shape))])
    return factor_of


def centred(own_key, shape, width, limit, shards=(), kind=jnp.bfloat16):
    values = jax.random.normal(own_key, shape, jnp.float32) * width
    if len(shards) > 0:
        values = steps_of(own_key, shape, shards, -0.22, 0.18) * values
    return jnp.clip(values, min=-limit, max=limit).astype(kind)


def setup_inputs(seed: int = 0) -> dict:
    key_list = jax.random.split(jax.random.key(seed), 5)
    integrals = centred(key_list[0], (N_AUX, N_ROW * N_COL * CAP, BLK, QDEV * BLK), 0.125, 0.75, ((0, 8), (1, 32)))
    block_mask = draw_block_mask(jax.random.fold_in(key_list[4], 71), 0)
    block_slots = draw_block_slots(jax.random.fold_in(key_list[4], 71), 0)
    orbitals = centred(key_list[3], (NOCC, NBAS), ((8.0 / (QDEV * N_AUX * NOCC)) ** 0.5), 0.107910156)
    return {"integrals": integrals, "block_mask": block_mask, "block_slots": block_slots, "orbitals": orbitals}


def half_transform(mask_tile, slot_tile, packed_tile, orbitals):
    capacity = packed_tile.shape[0]
    block_size = packed_tile.shape[1]
    row_blocks, block_count = mask_tile.shape
    occ_count = orbitals.shape[0]
    aux_count = packed_tile.shape[2] // block_size
    mask_flat = mask_tile.reshape(-1)
    slot_flat = slot_tile.reshape(-1)
    positions = jnp.arange(mask_flat.shape[0], dtype=jnp.int32)
    slot_ids = jnp.arange(capacity, dtype=jnp.int32)
    select = ((mask_flat[None, :] == 1) & (slot_flat[None, :] == slot_ids[:, None])).astype(jnp.int32)
    block_row = jnp.sum(select * (positions // block_count)[None, :], axis=1).astype(jnp.int32)
    lam_block = jnp.sum(select * (positions % block_count)[None, :], axis=1).astype(jnp.int32)
    present = jnp.sum(select, axis=1).astype(jnp.float32)
    weights = (block_row[:, None] == jnp.arange(row_blocks, dtype=jnp.int32)[None, :]).astype(jnp.float32) * present[:, None]
    orbital_blocks = jnp.take(orbitals.reshape(occ_count, block_count, block_size), lam_block, axis=1)
    products = jnp.einsum("isx,sxy->siy", orbital_blocks.astype(jnp.float32), packed_tile.astype(jnp.float32), precision=lax.Precision.HIGHEST)
    products = products.reshape(capacity, occ_count, aux_count, block_size)
    half_block = jnp.einsum("sb,siqm->iqbm", weights, products, precision=lax.Precision.HIGHEST)
    return half_block.reshape(occ_count, aux_count, row_blocks * block_size).astype(jnp.bfloat16)


def reference(integrals, block_mask, block_slots, orbitals):
    tiles = N_ROW * N_COL
    masks = block_mask.reshape(N_AUX, tiles, MB_DEV, NMB)
    slots = block_slots.reshape(N_AUX, tiles, MB_DEV, NMB)
    packed = integrals.reshape(N_AUX, tiles, CAP, BLK, QDEV * BLK)

    def per_batch(running_sum, batch_items):
        mask_batch, slot_batch, packed_batch = batch_items
        blocks = jax.vmap(half_transform, in_axes=(0, 0, 0, None))(mask_batch, slot_batch, packed_batch, orbitals)
        whole = jnp.transpose(blocks, (1, 2, 0, 3)).reshape(NOCC * QDEV, NBAS).astype(jnp.float32)
        return running_sum + jnp.dot(whole.T, whole, precision=lax.Precision.HIGHEST), None

    total, unused = lax.scan(per_batch, jnp.zeros((NBAS, NBAS), jnp.float32), (masks, slots, packed))
    return total.reshape(NBAS, N_ROW, NBAS // N_ROW)
```

```python
import functools

import jax
import jax.numpy as jnp
from jax import lax
from jax.experimental import pallas as pl
from jax.experimental.pallas import tpu as pltpu
from jax.sharding import PartitionSpec as P

VMEM_LIMIT = 48 * 1024 * 1024
CHUNKS = 4


def half_kernel(swap_ref, mask_ref, slot_ref, orb_ref, int_ref, whole_ref, a0_ref, a1_ref, b0_ref, b1_ref, place_ref, weight_ref):
    step = pl.program_id(0)
    occ = orb_ref.shape[0]
    capacity, block, lanes = int_ref.shape
    row_blocks, block_count = mask_ref.shape
    low = lax.broadcasted_iota(jnp.int32, (occ, 2 * block), 1) < block

    @pl.when(step == 0)
    def _():
        for s in range(capacity):
            place_ref[s] = -1
        for b in range(row_blocks):
            for l in range(block_count):
                slot = slot_ref[b, l]
                valid = (mask_ref[b, l] == 1) & (slot >= 0) & (slot < capacity)
                place_ref[jnp.where(valid, slot, capacity)] = b * block_count + l
        for pair in range(capacity // 2):
            parts = []
            for s in (2 * pair, 2 * pair + 1):
                place = place_ref[s]
                at = jnp.maximum(place, 0)
                b = at // block_count
                l = at % block_count
                columns = orb_ref[:, pl.ds(pl.multiple_of((l // 2) * (2 * block), 2 * block), 2 * block)].astype(jnp.float32)
                turned = pltpu.roll(columns, block, 1)
                value = jnp.where((l % 2) == (s % 2), columns, turned)
                parts.append((place, b, value))
            for b in range(row_blocks):
                chosen = [
                    jnp.where((place >= 0) & (home == b), value, 0.0) for place, home, value in parts
                ]
                weight_ref[b * occ : (b + 1) * occ, pair * 2 * block : (pair + 1) * 2 * block] = jnp.where(
                    low, chosen[0], chosen[1]
                ).astype(weight_ref.dtype)

    packed = int_ref[...].reshape(capacity * block, lanes)
    product = jnp.dot(weight_ref[...], packed, preferred_element_type=jnp.float32)
    pieces = []
    for pair in range(lanes // (2 * block)):
        first = product[:occ, pair * 2 * block : (pair + 1) * 2 * block]
        second = product[occ:, pair * 2 * block : (pair + 1) * 2 * block]
        pieces.append(jnp.where(low, first, pltpu.roll(second, block, 1)))
        pieces.append(jnp.where(low, pltpu.roll(first, block, 1), second))
    result = jnp.concatenate(pieces, axis=0).astype(whole_ref.dtype)
    whole_ref[...] = result
    swap = swap_ref[0]
    for target, out_ref in enumerate((a0_ref, a1_ref, b0_ref, b1_ref)):
        @pl.when(step == (target // 2) * 2 + ((target % 2) ^ swap))
        def _(out_ref=out_ref):
            out_ref[...] = result


def half_transform(swap, mask, slots, packed, orbitals):
    capacity, block, width = packed.shape
    occ = orbitals.shape[0]
    lanes = width // CHUNKS
    rows = lanes // block * occ
    chunk = jax.ShapeDtypeStruct((rows, 2 * block), jnp.bfloat16)
    smem = pl.BlockSpec(memory_space=pltpu.SMEM)
    fixed = pl.BlockSpec((rows, 2 * block), lambda g: (0, 0))
    return pl.pallas_call(
        half_kernel,
        grid=(CHUNKS,),
        out_shape=(jax.ShapeDtypeStruct((rows * CHUNKS, 2 * block), jnp.bfloat16),) + (chunk,) * 4,
        in_specs=[
            smem,
            smem,
            smem,
            pl.BlockSpec(orbitals.shape, lambda g: (0, 0)),
            pl.BlockSpec((capacity, block, lanes), lambda g: (0, 0, g)),
        ],
        out_specs=(pl.BlockSpec((rows, 2 * block), lambda g: (g, 0)),) + (fixed,) * 4,
        scratch_shapes=[
            pltpu.SMEM((capacity + 1,), jnp.int32),
            pltpu.VMEM((2 * occ, capacity * block), jnp.bfloat16),
        ],
        compiler_params=pltpu.CompilerParams(vmem_limit_bytes=VMEM_LIMIT),
        cost_estimate=pl.CostEstimate(flops=2 * 2 * occ * capacity * block * width, bytes_accessed=5 << 20, transcendentals=0),
    )(swap, mask, slots, orbitals, packed)


def columns_at(col_refs, start, rows):
    return jnp.concatenate([ref[pl.ds(start, rows), :] for ref in col_refs], axis=1)


CONTRACT = (((0,), (0,)), ((), ()))


def tiles_kernel(pos_ref, *refs):
    col_refs = refs[:4]
    moved = refs[4:16]
    out_ref = refs[16]
    col = pos_ref[0]
    rows = moved[0].shape[0]
    ring = out_ref.shape[0]
    own = None
    for part in range(4):
        term = lax.dot_general(
            col_refs[0][part * rows : (part + 1) * rows, :],
            columns_at(col_refs, part * rows, rows),
            CONTRACT,
            preferred_element_type=jnp.float32,
        )
        own = term if own is None else own + term
    out_ref[col] = own.astype(out_ref.dtype)
    for d in range(1, 4):
        for side in range(2):
            origin = lax.rem(col + (d if side == 0 else ring - d), ring)
            swap = (origin < ring // 2).astype(jnp.int32)
            total = None
            for part in range(2):
                start = pl.multiple_of((2 * side + (part ^ swap)) * rows, rows)
                term = lax.dot_general(
                    moved[(d - 1) * 4 + side * 2 + part][...],
                    columns_at(col_refs, start, rows),
                    CONTRACT,
                    preferred_element_type=jnp.float32,
                )
                total = term if total is None else total + term
            out_ref[origin] = total.astype(out_ref.dtype)


def tiles(pos, col_panels, moved, ring):
    rows, width = moved[0].shape
    return pl.pallas_call(
        tiles_kernel,
        out_shape=jax.ShapeDtypeStruct((ring, width, 4 * width), jnp.bfloat16),
        in_specs=[pl.BlockSpec(memory_space=pltpu.SMEM)] + [pl.BlockSpec(memory_space=pltpu.VMEM)] * 16,
        out_specs=pl.BlockSpec(memory_space=pltpu.VMEM),
        compiler_params=pltpu.CompilerParams(vmem_limit_bytes=VMEM_LIMIT),
        cost_estimate=pl.CostEstimate(flops=2 * width * 4 * width * rows * 16, bytes_accessed=7 << 20, transcendentals=0),
    )(pos, *col_panels, *moved)


def last_tile_kernel(pos_ref, old_ref, a_ref, b_ref, *refs):
    col_refs, out_ref = refs[:8], refs[8]
    total = None
    for side, ref in enumerate((a_ref, b_ref)):
        term = lax.dot_general(
            ref[...],
            jnp.concatenate([c[...] for c in col_refs[side * 4 : side * 4 + 4]], axis=1),
            CONTRACT,
            preferred_element_type=jnp.float32,
        )
        total = term if total is None else total + term
    out_ref[0] = total.astype(out_ref.dtype)


def last_tile(pos, sums, a_far, b_far, col_panels):
    ring, width, wide = sums.shape
    rows = a_far.shape[0]
    far = lambda pos: lax.rem(pos[0] + ring // 2, ring)
    swapped = lambda pos: (far(pos) < ring // 2).astype(jnp.int32)
    full = pl.BlockSpec((rows, width), lambda g, pos: (0, 0))
    col_specs = [
        pl.BlockSpec((rows, width), lambda g, pos, side=side: (2 * side + swapped(pos), 0))
        for side in range(2)
        for _ in range(4)
    ]
    return pl.pallas_call(
        last_tile_kernel,
        grid_spec=pltpu.PrefetchScalarGridSpec(
            num_scalar_prefetch=1,
            grid=(1,),
            in_specs=[pl.BlockSpec(memory_space=pl.ANY), full, full] + col_specs,
            out_specs=pl.BlockSpec((1, width, wide), lambda g, pos: (far(pos), 0, 0)),
        ),
        out_shape=jax.ShapeDtypeStruct(sums.shape, sums.dtype),
        input_output_aliases={1: 0},
        compiler_params=pltpu.CompilerParams(vmem_limit_bytes=VMEM_LIMIT),
        cost_estimate=pl.CostEstimate(flops=4 * width * wide * rows, bytes_accessed=2 << 20, transcendentals=0),
    )(pos, sums, a_far, b_far, *col_panels, *col_panels)


def sum_kernel(in_ref, *out_refs):
    total = in_ref[0].astype(jnp.float32)
    for a in range(1, in_ref.shape[0]):
        total = total + in_ref[a].astype(jnp.float32)
    width = out_refs[0].shape[1]
    for rho, ref in enumerate(out_refs):
        ref[...] = total[:, rho * width : (rho + 1) * width]


def sum_parts(received):
    count, width, wide = received.shape
    return pl.pallas_call(
        sum_kernel,
        out_shape=(jax.ShapeDtypeStruct((width, width), jnp.float32),) * (wide // width),
        compiler_params=pltpu.CompilerParams(vmem_limit_bytes=VMEM_LIMIT),
        cost_estimate=pl.CostEstimate(flops=count * width * wide, bytes_accessed=2 * count * width * wide, transcendentals=0),
    )(received)


def finish_kernel(pos_ref, *refs):
    own, other, out_ref = refs[:4], refs[4:8], refs[8]
    row = pos_ref[1]
    diagonal = pos_ref[0] == pos_ref[2]
    for rho in range(4):
        back = jnp.where(diagonal, 0.0, other[rho][...].T)
        out_ref[:, row ^ rho, :] = own[rho][...] + back


def finish(pos, own, other):
    width = own[0].shape[0]
    return pl.pallas_call(
        finish_kernel,
        out_shape=jax.ShapeDtypeStruct((width, 4, width), jnp.float32),
        in_specs=[pl.BlockSpec(memory_space=pltpu.SMEM)] + [pl.BlockSpec(memory_space=pltpu.VMEM)] * 8,
        out_specs=pl.BlockSpec(memory_space=pltpu.VMEM),
        compiler_params=pltpu.CompilerParams(vmem_limit_bytes=VMEM_LIMIT),
    )(pos, *own, *other)


def local(integrals, block_mask, block_slots, orbitals):
    row, col, aux = lax.axis_index("row"), lax.axis_index("col"), lax.axis_index("aux")
    ring, rows_n, aux_n = lax.axis_size("col"), lax.axis_size("row"), lax.axis_size("aux")
    pos = jnp.stack([col, row, aux]).astype(jnp.int32)
    swap = (col < ring // 2).astype(jnp.int32).reshape(1)
    whole, a0, a1, b0, b1 = half_transform(swap, block_mask[0], block_slots[0], integrals[0], orbitals)

    down = [(i, (i - 1) % ring) for i in range(ring)]
    up = [(i, (i + 1) % ring) for i in range(ring)]
    core = [(i, i ^ 1) for i in range(rows_n)]
    across = [(i, i ^ 2) for i in range(rows_n)]

    moved = []
    held = [a0, a1, b0, b1]
    for _ in range(3):
        held = [
            lax.ppermute(held[0], "col", down),
            lax.ppermute(held[1], "col", down),
            lax.ppermute(held[2], "col", up),
            lax.ppermute(held[3], "col", up),
        ]
        moved += held
    a_far = lax.ppermute(held[0], "col", down)
    b_far = lax.ppermute(held[2], "col", up)

    beside = lax.ppermute(whole, "row", core)
    over = lax.ppermute(whole, "row", across)
    diagonal = lax.ppermute(over, "row", core)
    col_panels = [whole, beside, over, diagonal]

    sums = tiles(pos, col_panels, moved, ring)
    sums = last_tile(pos, sums, a_far, b_far, col_panels)
    received = lax.all_to_all(sums, "aux", 0, 0, tiled=True)
    own = sum_parts(received)

    def flip(rho):
        return [
            ((r * ring + z) * aux_n + a, ((r ^ rho) * ring + a) * aux_n + z)
            for r in range(rows_n)
            for z in range(ring)
            for a in range(aux_n)
        ]

    other = [lax.ppermute(own[rho], ("row", "col", "aux"), flip(rho)) for rho in range(rows_n)]
    return finish(pos, own, other)


def solution(mesh):
    placed = (
        P("aux", ("row", "col"), None, None),
        P("aux", ("row", "col"), None),
        P("aux", ("row", "col"), None),
        P(),
    )
    return jax.shard_map(
        local, mesh=mesh, in_specs=placed, out_specs=P(("row", "aux"), None, "col"), check_vma=False
    )
```

```python
import functools

import jax
import jax.numpy as jnp
from jax import lax
from jax.experimental import pallas as pl
from jax.experimental.pallas import tpu as pltpu
from jax.sharding import PartitionSpec as P

WIDE_LIMIT = 60 * 1024 * 1024
VMEM_LIMIT = 16 * 1024 * 1024
CHUNKS = 4


def half_kernel(mask_ref, slot_ref, orb_ref, int_ref, whole_ref, lower_ref, upper_ref,
                place_ref, weight_ref, orb_buf, int_buf, out_buf, int_sem, orb_sem, out_sem, part_sem):
    chunks, capacity, block, lanes = int_buf.shape
    rows = out_buf.shape[1]
    occ = orb_buf.shape[0]
    row_blocks, block_count = mask_ref.shape
    low = lax.broadcasted_iota(jnp.int32, (occ, 2 * block), 1) < block

    def load(c):
        return pltpu.make_async_copy(int_ref.at[:, :, pl.ds(c * lanes, lanes)], int_buf.at[c], int_sem.at[c])

    orb_load = pltpu.make_async_copy(orb_ref, orb_buf, orb_sem)
    orb_load.start()
    for c in range(chunks):
        load(c).start()

    for s in range(capacity):
        place_ref[s] = -1
    for b in range(row_blocks):
        for l in range(block_count):
            slot = slot_ref[b, l]
            valid = (mask_ref[b, l] == 1) & (slot >= 0) & (slot < capacity)
            place_ref[jnp.where(valid, slot, capacity)] = b * block_count + l

    orb_load.wait()
    for pair in range(capacity // 2):
        parts = []
        for s in (2 * pair, 2 * pair + 1):
            place = place_ref[s]
            at = jnp.maximum(place, 0)
            home = at // block_count
            parity = lax.rem(at, 2)
            start = pl.multiple_of((lax.rem(at, block_count) // 2) * (2 * block), 2 * block)
            columns = orb_buf[:, pl.ds(start, 2 * block)].astype(jnp.float32)
            turned = pltpu.roll(columns, block, 1)
            value = jnp.where(parity == (s % 2), columns, turned)
            parts.append((place, home, value))
        for b in range(row_blocks):
            chosen = [jnp.where((place >= 0) & (home == b), value, 0.0) for place, home, value in parts]
            weight_ref[b * occ : (b + 1) * occ, pair * 2 * block : (pair + 1) * 2 * block] = jnp.where(
                low, chosen[0], chosen[1]
            ).astype(weight_ref.dtype)

    def store(c):
        return pltpu.make_async_copy(out_buf.at[c], whole_ref.at[pl.ds(c * rows, rows)], out_sem.at[c])

    def store_part(c):
        target = (lower_ref, upper_ref)[c // 2]
        return pltpu.make_async_copy(out_buf.at[c], target.at[pl.ds((c % 2) * rows, rows)], part_sem.at[c])

    for c in range(chunks):
        load(c).wait()
        packed = int_buf[c].reshape(capacity * block, lanes)
        product = jnp.dot(weight_ref[...], packed, preferred_element_type=jnp.float32)
        for pair in range(lanes // (2 * block)):
            first = product[:occ, pair * 2 * block : (pair + 1) * 2 * block]
            second = product[occ:, pair * 2 * block : (pair + 1) * 2 * block]
            out_buf[c, 2 * pair * occ : (2 * pair + 1) * occ, :] = jnp.where(
                low, first, pltpu.roll(second, block, 1)
            ).astype(out_buf.dtype)
            out_buf[c, (2 * pair + 1) * occ : (2 * pair + 2) * occ, :] = jnp.where(
                low, pltpu.roll(first, block, 1), second
            ).astype(out_buf.dtype)
        store_part(c).start()
        store(c).start()
    for c in range(chunks):
        store_part(c).wait()
        store(c).wait()


def half_transform(mask, slots, packed, orbitals):
    capacity, block, width = packed.shape
    occ = orbitals.shape[0]
    lanes = width // CHUNKS
    rows = lanes // block * occ
    smem = pl.BlockSpec(memory_space=pltpu.SMEM)
    anywhere = pl.BlockSpec(memory_space=pl.ANY)
    return pl.pallas_call(
        half_kernel,
        out_shape=(jax.ShapeDtypeStruct((rows * CHUNKS, 2 * block), jnp.bfloat16),)
        + (jax.ShapeDtypeStruct((rows * CHUNKS // 2, 2 * block), jnp.bfloat16),) * 2,
        in_specs=[smem, smem, anywhere, anywhere],
        out_specs=(anywhere,) * 3,
        scratch_shapes=[
            pltpu.SMEM((capacity + 1,), jnp.int32),
            pltpu.VMEM((2 * occ, capacity * block), jnp.bfloat16),
            pltpu.VMEM(orbitals.shape, jnp.bfloat16),
            pltpu.VMEM((CHUNKS, capacity, block, lanes), jnp.bfloat16),
            pltpu.VMEM((CHUNKS, rows, 2 * block), jnp.bfloat16),
            pltpu.SemaphoreType.DMA((CHUNKS,)),
            pltpu.SemaphoreType.DMA,
            pltpu.SemaphoreType.DMA((CHUNKS,)),
            pltpu.SemaphoreType.DMA((CHUNKS,)),
        ],
        compiler_params=pltpu.CompilerParams(vmem_limit_bytes=WIDE_LIMIT),
        cost_estimate=pl.CostEstimate(flops=2 * 2 * occ * capacity * block * width, bytes_accessed=5 << 20, transcendentals=0),
    )(mask, slots, orbitals, packed)


CONTRACT = (((0,), (0,)), ((), ()))


def tile_of(parts, col_refs):
    total, start = None, 0
    for ref in parts:
        rows = ref.shape[0]
        columns = jnp.concatenate([c[start : start + rows, :] for c in col_refs], axis=1)
        term = lax.dot_general(ref[...], columns, CONTRACT, preferred_element_type=jnp.float32)
        total = term if total is None else total + term
        start += rows
    return total


def early_kernel(count, *refs):
    col_refs, moved = refs[:4], refs[4 : 4 + 2 * count]
    out_ref, held, sems = refs[4 + 2 * count :]
    copies = [pltpu.make_async_copy(ref, held.at[n], sems.at[n]) for n, ref in enumerate(moved)]
    for copy in copies:
        copy.start()
    for n in range(count):
        copies[2 * n].wait()
        copies[2 * n + 1].wait()
        out_ref[n] = tile_of([held.at[2 * n], held.at[2 * n + 1]], col_refs).astype(out_ref.dtype)


def early_tiles(col_panels, moved):
    depth, width = col_panels[0].shape
    count = len(moved) // 2
    vmem = pl.BlockSpec(memory_space=pltpu.VMEM)
    return pl.pallas_call(
        functools.partial(early_kernel, count),
        out_shape=jax.ShapeDtypeStruct((count, width, 4 * width), jnp.bfloat16),
        in_specs=[vmem] * 4 + [pl.BlockSpec(memory_space=pltpu.HBM)] * (2 * count),
        out_specs=vmem,
        scratch_shapes=[
            pltpu.VMEM((2 * count,) + moved[0].shape, jnp.bfloat16),
            pltpu.SemaphoreType.DMA((2 * count,)),
        ],
        compiler_params=pltpu.CompilerParams(vmem_limit_bytes=VMEM_LIMIT),
        cost_estimate=pl.CostEstimate(flops=2 * width * 4 * width * depth * count, bytes_accessed=7 << 20, transcendentals=0),
    )(*col_panels, *moved)


def last_kernel(ring, pos_ref, *refs):
    done_refs, col_refs, parts, out_ref = refs[:3], refs[3:7], refs[7:9], refs[9]
    col = pos_ref[0]

    def origin(d):
        return lax.rem(col + d, ring)

    for ref, distances in zip(done_refs, ((0, 1, ring - 1), (2, ring - 2), (3, ring - 3))):
        for n, d in enumerate(distances):
            out_ref[origin(d)] = ref[n]
    out_ref[origin(4)] = tile_of(parts, col_refs).astype(out_ref.dtype)


def last_tile(pos, done, col_panels, parts, ring):
    depth, width = col_panels[0].shape
    return pl.pallas_call(
        functools.partial(last_kernel, ring),
        out_shape=jax.ShapeDtypeStruct((ring, width, 4 * width), jnp.bfloat16),
        in_specs=[pl.BlockSpec(memory_space=pltpu.SMEM)] + [pl.BlockSpec(memory_space=pltpu.VMEM)] * 9,
        out_specs=pl.BlockSpec(memory_space=pltpu.VMEM),
        compiler_params=pltpu.CompilerParams(vmem_limit_bytes=VMEM_LIMIT),
        cost_estimate=pl.CostEstimate(flops=2 * width * 4 * width * depth, bytes_accessed=6 << 20, transcendentals=0),
    )(pos, *done, *col_panels, *parts)


def sum_kernel(pos_ref, in_ref, out_ref):
    width = out_ref.shape[2]
    for rho in range(out_ref.shape[1]):
        total = None
        for a in range(in_ref.shape[0]):
            term = in_ref[a, :, rho * width : (rho + 1) * width].astype(jnp.float32)
            total = term if total is None else total + term
        out_ref[:, pos_ref[1] ^ rho, :] = total


def sum_parts(pos, received):
    count, width, wide = received.shape
    return pl.pallas_call(
        sum_kernel,
        out_shape=jax.ShapeDtypeStruct((width, wide // width, width), jnp.float32),
        in_specs=[pl.BlockSpec(memory_space=pltpu.SMEM), pl.BlockSpec(memory_space=pltpu.VMEM)],
        out_specs=pl.BlockSpec(memory_space=pltpu.VMEM),
        compiler_params=pltpu.CompilerParams(vmem_limit_bytes=VMEM_LIMIT),
        cost_estimate=pl.CostEstimate(flops=count * width * wide, bytes_accessed=2 * count * width * wide, transcendentals=0),
    )(pos, received)


def local(integrals, block_mask, block_slots, orbitals):
    row, col = lax.axis_index("row"), lax.axis_index("col")
    ring, rows_n = lax.axis_size("col"), lax.axis_size("row")
    pos = jnp.stack([col, row]).astype(jnp.int32)
    whole, lower, upper = half_transform(block_mask[0], block_slots[0], integrals[0], orbitals)

    down = [(i, (i - 1) % ring) for i in range(ring)]
    up = [(i, (i + 1) % ring) for i in range(ring)]

    def hop(held):
        return [
            lax.ppermute(held[0], "col", down),
            lax.ppermute(held[1], "col", down),
            lax.ppermute(held[2], "col", up),
            lax.ppermute(held[3], "col", up),
        ]

    beside = lax.ppermute(whole, "row", [(i, i ^ 1) for i in range(rows_n)])
    over = lax.ppermute(whole, "row", [(i, i ^ 2) for i in range(rows_n)])
    first = hop([lower, upper, lower, upper])
    over, first[1] = lax.optimization_barrier((over, first[1]))
    second = hop(first)
    diagonal = lax.ppermute(over, "row", [(i, i ^ 1) for i in range(rows_n)])
    col_panels = [whole, beside, over, diagonal]
    near = early_tiles(col_panels, [lower, upper] + first)
    near, second[2] = lax.optimization_barrier((near, second[2]))
    third = hop(second)
    middle = early_tiles(col_panels, second)
    middle, third[0] = lax.optimization_barrier((middle, third[0]))
    parts = [lax.ppermute(third[0], "col", down), lax.ppermute(third[3], "col", up)]
    outer = early_tiles(col_panels, third)
    sums = last_tile(pos, [near, middle, outer], col_panels, parts, ring)
    received = lax.all_to_all(sums, "aux", 0, 0, tiled=True)
    return sum_parts(pos, received)


def solution(mesh):
    placed = (
        P("aux", ("row", "col"), None, None),
        P("aux", ("row", "col"), None),
        P("aux", ("row", "col"), None),
        P(),
    )
    return jax.shard_map(
        local, mesh=mesh, in_specs=placed, out_specs=P(("row", "aux"), None, "col"), check_vma=False
    )
```

```python
import functools

import jax
import jax.numpy as jnp
from jax import lax
from jax.experimental import pallas as pl
from jax.experimental.pallas import tpu as pltpu
from jax.sharding import PartitionSpec as P

WIDE_LIMIT = 60 * 1024 * 1024
VMEM_LIMIT = 16 * 1024 * 1024
CHUNKS = 2


def half_kernel(mask_ref, slot_ref, orb_ref, int_ref, whole_ref,
                place_ref, weight_ref, orb_buf, int_buf, out_buf, int_sem, orb_sem, out_sem):
    chunks, capacity, block, lanes = int_buf.shape
    rows = out_buf.shape[1]
    occ = orb_buf.shape[0]
    row_blocks, block_count = mask_ref.shape
    low = lax.broadcasted_iota(jnp.int32, (occ, 2 * block), 1) < block

    def load(c):
        return pltpu.make_async_copy(int_ref.at[:, :, pl.ds(c * lanes, lanes)], int_buf.at[c], int_sem.at[c])

    orb_load = pltpu.make_async_copy(orb_ref, orb_buf, orb_sem)
    orb_load.start()
    for c in range(chunks):
        load(c).start()

    position = lax.broadcasted_iota(jnp.int32, mask_ref.shape, 0) * block_count + lax.broadcasted_iota(
        jnp.int32, mask_ref.shape, 1
    )
    slots = jnp.where(mask_ref[...] == 1, slot_ref[...], -1)
    for s in range(capacity):
        place_ref[s] = jnp.max(jnp.where(slots == s, position, -1))

    orb_load.wait()
    for pair in range(capacity // 2):
        parts = []
        for s in (2 * pair, 2 * pair + 1):
            place = place_ref[s]
            at = jnp.maximum(place, 0)
            home = at // block_count
            parity = lax.rem(at, 2)
            start = pl.multiple_of((lax.rem(at, block_count) // 2) * (2 * block), 2 * block)
            columns = orb_buf[:, pl.ds(start, 2 * block)].astype(jnp.float32)
            turned = pltpu.roll(columns, block, 1)
            value = jnp.where(parity == (s % 2), columns, turned)
            parts.append((place, home, value))
        for b in range(row_blocks):
            chosen = [jnp.where((place >= 0) & (home == b), value, 0.0) for place, home, value in parts]
            weight_ref[b * occ : (b + 1) * occ, pair * 2 * block : (pair + 1) * 2 * block] = jnp.where(
                low, chosen[0], chosen[1]
            ).astype(weight_ref.dtype)

    def store(c):
        return pltpu.make_async_copy(out_buf.at[c], whole_ref.at[pl.ds(c * rows, rows)], out_sem.at[c])

    for c in range(chunks):
        load(c).wait()
        packed = int_buf[c].reshape(capacity * block, lanes)
        product = jnp.dot(weight_ref[...], packed, preferred_element_type=jnp.float32)
        for pair in range(lanes // (2 * block)):
            first = product[:occ, pair * 2 * block : (pair + 1) * 2 * block]
            second = product[occ:, pair * 2 * block : (pair + 1) * 2 * block]
            out_buf[c, 2 * pair * occ : (2 * pair + 1) * occ, :] = jnp.where(
                low, first, pltpu.roll(second, block, 1)
            ).astype(out_buf.dtype)
            out_buf[c, (2 * pair + 1) * occ : (2 * pair + 2) * occ, :] = jnp.where(
                low, pltpu.roll(first, block, 1), second
            ).astype(out_buf.dtype)
        store(c).start()
    for c in range(chunks):
        store(c).wait()


def half_transform(mask, slots, packed, orbitals):
    capacity, block, width = packed.shape
    occ = orbitals.shape[0]
    lanes = width // CHUNKS
    rows = lanes // block * occ
    vmem = pl.BlockSpec(memory_space=pltpu.VMEM)
    anywhere = pl.BlockSpec(memory_space=pl.ANY)
    return pl.pallas_call(
        half_kernel,
        out_shape=jax.ShapeDtypeStruct((rows * CHUNKS, 2 * block), jnp.bfloat16),
        in_specs=[vmem, vmem, anywhere, anywhere],
        out_specs=anywhere,
        scratch_shapes=[
            pltpu.SMEM((capacity,), jnp.int32),
            pltpu.VMEM((2 * occ, capacity * block), jnp.bfloat16),
            pltpu.VMEM(orbitals.shape, jnp.bfloat16),
            pltpu.VMEM((CHUNKS, capacity, block, lanes), jnp.bfloat16),
            pltpu.VMEM((CHUNKS, rows, 2 * block), jnp.bfloat16),
            pltpu.SemaphoreType.DMA((CHUNKS,)),
            pltpu.SemaphoreType.DMA,
            pltpu.SemaphoreType.DMA((CHUNKS,)),
        ],
        compiler_params=pltpu.CompilerParams(vmem_limit_bytes=WIDE_LIMIT),
        cost_estimate=pl.CostEstimate(flops=2 * 2 * occ * capacity * block * width, bytes_accessed=5 << 20, transcendentals=0),
    )(mask, slots, orbitals, packed)


CONTRACT = (((0,), (0,)), ((), ()))


def tile_of(parts, col_refs):
    total, start = None, 0
    for ref in parts:
        rows = ref.shape[0]
        columns = jnp.concatenate([c[start : start + rows, :] for c in col_refs], axis=1)
        term = lax.dot_general(ref[...], columns, CONTRACT, preferred_element_type=jnp.float32)
        total = term if total is None else total + term
        start += rows
    return total


def early_kernel(orders, *refs):
    count = len(orders)
    col_refs, moved = refs[:4], refs[4 : 4 + count]
    out_refs = refs[4 + count : -2]
    held, sems = refs[-2:]
    copies = [pltpu.make_async_copy(ref, held.at[n], sems.at[n]) for n, ref in enumerate(moved)]
    for copy in copies:
        copy.start()
    filled = [0, 0]
    for n, (group, order) in enumerate(orders):
        copies[n].wait()
        tile = tile_of([held.at[n]], [col_refs[o] for o in order])
        out_refs[group][filled[group]] = tile.astype(out_refs[group].dtype)
        filled[group] += 1


def early_tiles(col_panels, kept, sent):
    depth, width = col_panels[0].shape
    orders = [(0, (0, 1, 2, 3))] * len(kept) + [(1, (1, 0, 3, 2))] * len(sent)
    vmem = pl.BlockSpec(memory_space=pltpu.VMEM)
    return pl.pallas_call(
        functools.partial(early_kernel, orders),
        out_shape=tuple(
            jax.ShapeDtypeStruct((len(group), width, 4 * width), jnp.bfloat16) for group in (kept, sent)
        ),
        in_specs=[vmem] * 4 + [pl.BlockSpec(memory_space=pl.ANY)] * len(orders),
        out_specs=(vmem, vmem),
        scratch_shapes=[
            pltpu.VMEM((len(orders), depth, width), jnp.bfloat16),
            pltpu.SemaphoreType.DMA((len(orders),)),
        ],
        compiler_params=pltpu.CompilerParams(vmem_limit_bytes=VMEM_LIMIT),
        cost_estimate=pl.CostEstimate(flops=8 * width * width * depth * len(orders), bytes_accessed=7 << 20, transcendentals=0),
    )(*col_panels, *kept, *sent)


def last_kernel(ring, *refs):
    col_refs, far_ref, out_ref = refs[4:8], refs[8], refs[9]
    near_ref, outer_ref, near_other_ref, outer_other_ref = refs[:4]
    col, core = lax.axis_index("col"), lax.rem(lax.axis_index("row"), 2)

    def origin(d):
        return lax.rem(col + jnp.where(core == 0, d, ring - d), ring)

    for d in range(3):
        out_ref[origin(d)] = near_ref[d]
    out_ref[origin(3)] = outer_ref[0]
    for d in range(1, 3):
        out_ref[origin(ring - d)] = near_other_ref[d - 1]
    out_ref[origin(ring - 3)] = outer_other_ref[0]
    out_ref[origin(4)] = tile_of([far_ref], col_refs).astype(out_ref.dtype)


def last_tile(done, col_panels, far, ring):
    depth, width = far.shape
    return pl.pallas_call(
        functools.partial(last_kernel, ring),
        out_shape=jax.ShapeDtypeStruct((ring, width, 4 * width), jnp.bfloat16),
        in_specs=[pl.BlockSpec(memory_space=pltpu.VMEM)] * 9,
        out_specs=pl.BlockSpec(memory_space=pltpu.VMEM),
        compiler_params=pltpu.CompilerParams(vmem_limit_bytes=VMEM_LIMIT),
        cost_estimate=pl.CostEstimate(flops=8 * width * width * depth, bytes_accessed=6 << 20, transcendentals=0),
    )(*done, *col_panels, far)


def sum_kernel(in_ref, out_ref):
    row = lax.axis_index("row")
    width = out_ref.shape[2]
    for rho in range(out_ref.shape[1]):
        total = None
        for a in range(in_ref.shape[0]):
            term = in_ref[a, :, rho * width : (rho + 1) * width].astype(jnp.float32)
            total = term if total is None else total + term
        out_ref[:, row ^ rho, :] = total


def sum_parts(received):
    count, width, wide = received.shape
    return pl.pallas_call(
        sum_kernel,
        out_shape=jax.ShapeDtypeStruct((width, wide // width, width), jnp.float32),
        in_specs=[pl.BlockSpec(memory_space=pltpu.VMEM)],
        out_specs=pl.BlockSpec(memory_space=pltpu.VMEM),
        compiler_params=pltpu.CompilerParams(vmem_limit_bytes=VMEM_LIMIT),
        cost_estimate=pl.CostEstimate(flops=count * width * wide, bytes_accessed=2 * count * width * wide, transcendentals=0),
    )(received)


def local(integrals, block_mask, block_slots, orbitals):
    ring, rows_n = lax.axis_size("col"), lax.axis_size("row")
    whole = half_transform(block_mask[0], block_slots[0], integrals[0], orbitals)

    along = [
        (r * ring + z, r * ring + (z + (ring - 1 if r % 2 == 0 else 1)) % ring)
        for r in range(rows_n)
        for z in range(ring)
    ]

    def hop(panel):
        return lax.ppermute(panel, ("row", "col"), along)

    def to_row(value, rho):
        return lax.ppermute(value, "row", [(i, i ^ rho) for i in range(rows_n)])

    kept = [whole, hop(whole)]
    beside = to_row(whole, 1)
    over = to_row(whole, 2)
    sent = [hop(beside)]
    kept.append(hop(kept[1]))
    sent.append(hop(sent[0]))
    over, kept[2] = lax.optimization_barrier((over, kept[2]))
    diagonal = to_row(over, 1)
    col_panels = [whole, beside, over, diagonal]
    near = early_tiles(col_panels, kept, sent)
    third = hop(kept[2])
    third_sent = hop(sent[1])
    near_kept, near_sent, third = lax.optimization_barrier((*near, third))
    far = hop(third)
    near_other = to_row(near_sent, 1)
    outer_kept, outer_sent = early_tiles(col_panels, [third], [third_sent])
    outer_other = to_row(outer_sent, 1)
    sums = last_tile([near_kept, outer_kept, near_other, outer_other], col_panels, far, ring)
    received = lax.all_to_all(sums, "aux", 0, 0, tiled=True)
    return sum_parts(received)


def solution(mesh):
    placed = (
        P("aux", ("row", "col"), None, None),
        P("aux", ("row", "col"), None),
        P("aux", ("row", "col"), None),
        P(),
    )
    return jax.shard_map(
        local, mesh=mesh, in_specs=placed, out_specs=P(("row", "aux"), None, "col"), check_vma=False
    )
```

```python
import functools

import jax
import jax.numpy as jnp
from jax import lax
from jax.experimental import pallas as pl
from jax.experimental.pallas import tpu as pltpu
from jax.sharding import PartitionSpec as P

WIDE_LIMIT = 60 * 1024 * 1024
VMEM_LIMIT = 16 * 1024 * 1024
CHUNKS = 2


def half_kernel(mask_ref, slot_ref, orb_ref, int_ref, whole_ref,
                place_ref, weight_ref, orb_buf, int_buf, out_buf, int_sem, orb_sem, out_sem):
    chunks, capacity, block, lanes = int_buf.shape
    rows = out_buf.shape[1]
    occ = orb_buf.shape[0]
    row_blocks, block_count = mask_ref.shape
    low = lax.broadcasted_iota(jnp.int32, (occ, 2 * block), 1) < block

    def load(c):
        return pltpu.make_async_copy(int_ref.at[:, :, pl.ds(c * lanes, lanes)], int_buf.at[c], int_sem.at[c])

    orb_load = pltpu.make_async_copy(orb_ref, orb_buf, orb_sem)
    orb_load.start()
    for c in range(chunks):
        load(c).start()

    position = lax.broadcasted_iota(jnp.int32, mask_ref.shape, 0) * block_count + lax.broadcasted_iota(
        jnp.int32, mask_ref.shape, 1
    )
    slots = jnp.where(mask_ref[...] == 1, slot_ref[...], -1)
    for s in range(capacity):
        place_ref[s] = jnp.max(jnp.where(slots == s, position, -1))

    orb_load.wait()
    for pair in range(capacity // 2):
        parts = []
        for s in (2 * pair, 2 * pair + 1):
            place = place_ref[s]
            at = jnp.maximum(place, 0)
            home = at // block_count
            parity = lax.rem(at, 2)
            start = pl.multiple_of((lax.rem(at, block_count) // 2) * (2 * block), 2 * block)
            columns = orb_buf[:, pl.ds(start, 2 * block)].astype(jnp.float32)
            turned = pltpu.roll(columns, block, 1)
            value = jnp.where(parity == (s % 2), columns, turned)
            parts.append((place, home, value))
        for b in range(row_blocks):
            chosen = [jnp.where((place >= 0) & (home == b), value, 0.0) for place, home, value in parts]
            weight_ref[b * occ : (b + 1) * occ, pair * 2 * block : (pair + 1) * 2 * block] = jnp.where(
                low, chosen[0], chosen[1]
            ).astype(weight_ref.dtype)

    def store(c):
        return pltpu.make_async_copy(out_buf.at[c], whole_ref.at[pl.ds(c * rows, rows)], out_sem.at[c])

    for c in range(chunks):
        load(c).wait()
        packed = int_buf[c].reshape(capacity * block, lanes)
        product = jnp.dot(weight_ref[...], packed, preferred_element_type=jnp.float32)
        for pair in range(lanes // (2 * block)):
            first = product[:occ, pair * 2 * block : (pair + 1) * 2 * block]
            second = product[occ:, pair * 2 * block : (pair + 1) * 2 * block]
            out_buf[c, 2 * pair * occ : (2 * pair + 1) * occ, :] = jnp.where(
                low, first, pltpu.roll(second, block, 1)
            ).astype(out_buf.dtype)
            out_buf[c, (2 * pair + 1) * occ : (2 * pair + 2) * occ, :] = jnp.where(
                low, pltpu.roll(first, block, 1), second
            ).astype(out_buf.dtype)
        store(c).start()
    for c in range(chunks):
        store(c).wait()


def half_transform(mask, slots, packed, orbitals):
    capacity, block, width = packed.shape
    occ = orbitals.shape[0]
    lanes = width // CHUNKS
    rows = lanes // block * occ
    vmem = pl.BlockSpec(memory_space=pltpu.VMEM)
    anywhere = pl.BlockSpec(memory_space=pl.ANY)
    return pl.pallas_call(
        half_kernel,
        out_shape=jax.ShapeDtypeStruct((rows * CHUNKS, 2 * block), jnp.bfloat16),
        in_specs=[vmem, vmem, anywhere, anywhere],
        out_specs=anywhere,
        scratch_shapes=[
            pltpu.SMEM((capacity,), jnp.int32),
            pltpu.VMEM((2 * occ, capacity * block), jnp.bfloat16),
            pltpu.VMEM(orbitals.shape, jnp.bfloat16),
            pltpu.VMEM((CHUNKS, capacity, block, lanes), jnp.bfloat16),
            pltpu.VMEM((CHUNKS, rows, 2 * block), jnp.bfloat16),
            pltpu.SemaphoreType.DMA((CHUNKS,)),
            pltpu.SemaphoreType.DMA,
            pltpu.SemaphoreType.DMA((CHUNKS,)),
        ],
        compiler_params=pltpu.CompilerParams(vmem_limit_bytes=WIDE_LIMIT),
        cost_estimate=pl.CostEstimate(flops=2 * 2 * occ * capacity * block * width, bytes_accessed=5 << 20, transcendentals=0),
    )(mask, slots, orbitals, packed)


CONTRACT = (((0,), (0,)), ((), ()))


def tile_of(parts, col_refs):
    total, start = None, 0
    for ref in parts:
        rows = ref.shape[0]
        columns = jnp.concatenate([c[start : start + rows, :] for c in col_refs], axis=1)
        term = lax.dot_general(ref[...], columns, CONTRACT, preferred_element_type=jnp.float32)
        total = term if total is None else total + term
        start += rows
    return total


def packed_diagonal(square):
    size = square.shape[0]
    row = lax.broadcasted_iota(jnp.int32, square.shape, 0)
    column = lax.broadcasted_iota(jnp.int32, square.shape, 1)
    left = square - square.astype(jnp.bfloat16).astype(jnp.float32)
    left = jnp.sum(jnp.where(row == column, left, 0.0), axis=0, keepdims=True)
    final = jnp.sum(jnp.where(column[:1] == size - 1, left, 0.0), axis=1, keepdims=True)
    left = jnp.where((row == size - 1) & (column == 0), final, left)
    return jnp.where(row > column, left, square)


def unpacked_diagonal(square):
    size = square.shape[0]
    row = lax.broadcasted_iota(jnp.int32, square.shape, 0)
    column = lax.broadcasted_iota(jnp.int32, square.shape, 1)
    bottom = square[size - 1 :, :]
    final = jnp.sum(jnp.where(column[:1] == 0, bottom, 0.0), axis=1, keepdims=True)
    left = jnp.where(column[:1] == 0, square[size - 2 : size - 1, :], bottom)
    left = jnp.where(column[:1] == size - 1, final, left)
    whole = jnp.where(row > column, square.T, square)
    return jnp.where(row == column, square + left, whole)


def early_kernel(orders, own, *refs):
    count = len(orders)
    col_refs, moved = refs[:4], refs[4 : 4 + count]
    out_refs = refs[4 + count : -2]
    held, sems = refs[-2:]
    copies = [pltpu.make_async_copy(ref, held.at[n], sems.at[n]) for n, ref in enumerate(moved)]
    for copy in copies:
        copy.start()
    filled = [0, 0]
    for n, (group, order) in enumerate(orders):
        copies[n].wait()
        tile = tile_of([held.at[n]], [col_refs[o] for o in order])
        if own and n == 0:
            size = tile.shape[0]
            tile = jnp.concatenate([packed_diagonal(tile[:, :size]), tile[:, size:]], axis=1)
        out_refs[group][filled[group]] = tile.astype(out_refs[group].dtype)
        filled[group] += 1


def early_tiles(col_panels, kept, sent, own):
    depth, width = col_panels[0].shape
    orders = [(0, (0, 1, 2, 3))] * len(kept) + [(1, (1, 0, 3, 2))] * len(sent)
    vmem = pl.BlockSpec(memory_space=pltpu.VMEM)
    return pl.pallas_call(
        functools.partial(early_kernel, orders, own),
        out_shape=tuple(
            jax.ShapeDtypeStruct((len(group), width, 4 * width), jnp.bfloat16) for group in (kept, sent)
        ),
        in_specs=[vmem] * 4 + [pl.BlockSpec(memory_space=pl.ANY)] * len(orders),
        out_specs=(vmem, vmem),
        scratch_shapes=[
            pltpu.VMEM((len(orders), depth, width), jnp.bfloat16),
            pltpu.SemaphoreType.DMA((len(orders),)),
        ],
        compiler_params=pltpu.CompilerParams(vmem_limit_bytes=VMEM_LIMIT),
        cost_estimate=pl.CostEstimate(flops=8 * width * width * depth * len(orders), bytes_accessed=7 << 20, transcendentals=0),
    )(*col_panels, *kept, *sent)


def last_kernel(ring, *refs):
    col_refs, far_ref, out_ref = refs[4:8], refs[8], refs[9]
    near_ref, outer_ref, near_other_ref, outer_other_ref = refs[:4]
    col, core = lax.axis_index("col"), lax.rem(lax.axis_index("row"), 2)

    def origin(d):
        return lax.rem(col + jnp.where(core == 0, d, ring - d), ring)

    for d in range(3):
        out_ref[origin(d)] = near_ref[d]
    out_ref[origin(3)] = outer_ref[0]
    for d in range(1, 3):
        out_ref[origin(ring - d)] = near_other_ref[d - 1]
    out_ref[origin(ring - 3)] = outer_other_ref[0]
    out_ref[origin(4)] = tile_of([far_ref], col_refs).astype(out_ref.dtype)


def last_tile(done, col_panels, far, ring):
    depth, width = far.shape
    return pl.pallas_call(
        functools.partial(last_kernel, ring),
        out_shape=jax.ShapeDtypeStruct((ring, width, 4 * width), jnp.bfloat16),
        in_specs=[pl.BlockSpec(memory_space=pltpu.VMEM)] * 9,
        out_specs=pl.BlockSpec(memory_space=pltpu.VMEM),
        compiler_params=pltpu.CompilerParams(vmem_limit_bytes=VMEM_LIMIT),
        cost_estimate=pl.CostEstimate(flops=8 * width * width * depth, bytes_accessed=6 << 20, transcendentals=0),
    )(*done, *col_panels, far)


def sum_kernel(in_ref, out_ref):
    row = lax.axis_index("row")
    width = out_ref.shape[2]
    for rho in range(out_ref.shape[1]):
        total = None
        for a in range(in_ref.shape[0]):
            term = in_ref[a, :, rho * width : (rho + 1) * width].astype(jnp.float32)
            total = term if total is None else total + term
        out_ref[:, row ^ rho, :] = total
        if rho == 0:
            @pl.when(lax.axis_index("aux") == lax.axis_index("col"))
            def _(total=total):
                out_ref[:, row, :] = unpacked_diagonal(total)


def sum_parts(received):
    count, width, wide = received.shape
    return pl.pallas_call(
        sum_kernel,
        out_shape=jax.ShapeDtypeStruct((width, wide // width, width), jnp.float32),
        in_specs=[pl.BlockSpec(memory_space=pltpu.VMEM)],
        out_specs=pl.BlockSpec(memory_space=pltpu.VMEM),
        compiler_params=pltpu.CompilerParams(vmem_limit_bytes=VMEM_LIMIT),
        cost_estimate=pl.CostEstimate(flops=count * width * wide, bytes_accessed=2 * count * width * wide, transcendentals=0),
    )(received)


def local(integrals, block_mask, block_slots, orbitals):
    ring, rows_n = lax.axis_size("col"), lax.axis_size("row")
    whole = half_transform(block_mask[0], block_slots[0], integrals[0], orbitals)

    along = [
        (r * ring + z, r * ring + (z + (ring - 1 if r % 2 == 0 else 1)) % ring)
        for r in range(rows_n)
        for z in range(ring)
    ]

    def hop(panel):
        return lax.ppermute(panel, ("row", "col"), along)

    def to_row(value, rho):
        return lax.ppermute(value, "row", [(i, i ^ rho) for i in range(rows_n)])

    kept = [whole, hop(whole)]
    beside = to_row(whole, 1)
    over = to_row(whole, 2)
    sent = [hop(beside)]
    kept.append(hop(kept[1]))
    sent.append(hop(sent[0]))
    over, kept[2] = lax.optimization_barrier((over, kept[2]))
    diagonal = to_row(over, 1)
    col_panels = [whole, beside, over, diagonal]
    near = early_tiles(col_panels, kept, sent, True)
    third = hop(kept[2])
    third_sent = hop(sent[1])
    near_kept, near_sent, third = lax.optimization_barrier((*near, third))
    far = hop(third)
    near_other = to_row(near_sent, 1)
    outer_kept, outer_sent = early_tiles(col_panels, [third], [third_sent], False)
    outer_other = to_row(outer_sent, 1)
    sums = last_tile([near_kept, outer_kept, near_other, outer_other], col_panels, far, ring)
    received = lax.all_to_all(sums, "aux", 0, 0, tiled=True)
    return sum_parts(received)


def solution(mesh):
    placed = (
        P("aux", ("row", "col"), None, None),
        P("aux", ("row", "col"), None),
        P("aux", ("row", "col"), None),
        P(),
    )
    return jax.shard_map(
        local, mesh=mesh, in_specs=placed, out_specs=P(("row", "aux"), None, "col"), check_vma=False
    )
```

```python
import functools

import jax
import jax.numpy as jnp
from jax import lax
from jax.experimental import pallas as pl
from jax.experimental.pallas import tpu as pltpu
from jax.sharding import PartitionSpec as P

WIDE_LIMIT = 60 * 1024 * 1024
VMEM_LIMIT = 16 * 1024 * 1024
CHUNKS = ((0, 2), (2, 1))
THIRDS = 3


def half_kernel(mask_ref, slot_ref, orb_ref, int_ref, whole_ref,
                place_ref, weight_ref, orb_buf, int_buf, out_buf, int_sem, orb_sem, out_sem):
    capacity, block, width = int_buf.shape
    lanes, rows = width // THIRDS, out_buf.shape[0] // THIRDS
    occ = orb_buf.shape[0]
    row_blocks, block_count = mask_ref.shape
    low = lax.broadcasted_iota(jnp.int32, (occ, 2 * block), 1) < block

    def load(c):
        part = pl.ds(CHUNKS[c][0] * lanes, CHUNKS[c][1] * lanes)
        return pltpu.make_async_copy(int_ref.at[:, :, part], int_buf.at[:, :, part], int_sem.at[c])

    orb_load = pltpu.make_async_copy(orb_ref, orb_buf, orb_sem)
    orb_load.start()
    for c in range(len(CHUNKS)):
        load(c).start()

    position = lax.broadcasted_iota(jnp.int32, mask_ref.shape, 0) * block_count + lax.broadcasted_iota(
        jnp.int32, mask_ref.shape, 1
    )
    slots = jnp.where(mask_ref[...] == 1, slot_ref[...], -1)
    for s in range(capacity):
        place_ref[s] = jnp.max(jnp.where(slots == s, position, -1))

    orb_load.wait()
    for pair in range(capacity // 2):
        parts = []
        for s in (2 * pair, 2 * pair + 1):
            place = place_ref[s]
            at = jnp.maximum(place, 0)
            home = at // block_count
            parity = lax.rem(at, 2)
            start = pl.multiple_of((lax.rem(at, block_count) // 2) * (2 * block), 2 * block)
            columns = orb_buf[:, pl.ds(start, 2 * block)].astype(jnp.float32)
            turned = pltpu.roll(columns, block, 1)
            value = jnp.where(parity == (s % 2), columns, turned)
            parts.append((place, home, value))
        for b in range(row_blocks):
            chosen = [jnp.where((place >= 0) & (home == b), value, 0.0) for place, home, value in parts]
            weight_ref[b * occ : (b + 1) * occ, pair * 2 * block : (pair + 1) * 2 * block] = jnp.where(
                low, chosen[0], chosen[1]
            ).astype(weight_ref.dtype)

    def store(n):
        part = pl.ds(n * rows, rows)
        return pltpu.make_async_copy(out_buf.at[part], whole_ref.at[part], out_sem.at[n])

    for c, (begin, count) in enumerate(CHUNKS):
        load(c).wait()
        for n in range(begin, begin + count):
            packed = int_buf[:, :, n * lanes : (n + 1) * lanes].reshape(capacity * block, lanes)
            product = jnp.dot(weight_ref[...], packed, preferred_element_type=jnp.float32)
            for pair in range(lanes // (2 * block)):
                first = product[:occ, pair * 2 * block : (pair + 1) * 2 * block]
                second = product[occ:, pair * 2 * block : (pair + 1) * 2 * block]
                at = n * rows + 2 * pair * occ
                out_buf[at : at + occ, :] = jnp.where(low, first, pltpu.roll(second, block, 1)).astype(out_buf.dtype)
                out_buf[at + occ : at + 2 * occ, :] = jnp.where(
                    low, pltpu.roll(first, block, 1), second
                ).astype(out_buf.dtype)
            store(n).start()
    for n in range(THIRDS):
        store(n).wait()


def half_transform(mask, slots, packed, orbitals):
    capacity, block, width = packed.shape
    occ = orbitals.shape[0]
    rows = width // block * occ
    vmem = pl.BlockSpec(memory_space=pltpu.VMEM)
    anywhere = pl.BlockSpec(memory_space=pl.ANY)
    return pl.pallas_call(
        half_kernel,
        out_shape=jax.ShapeDtypeStruct((rows, 2 * block), jnp.bfloat16),
        in_specs=[vmem, vmem, anywhere, anywhere],
        out_specs=anywhere,
        scratch_shapes=[
            pltpu.SMEM((capacity,), jnp.int32),
            pltpu.VMEM((2 * occ, capacity * block), jnp.bfloat16),
            pltpu.VMEM(orbitals.shape, jnp.bfloat16),
            pltpu.VMEM(packed.shape, jnp.bfloat16),
            pltpu.VMEM((rows, 2 * block), jnp.bfloat16),
            pltpu.SemaphoreType.DMA((len(CHUNKS),)),
            pltpu.SemaphoreType.DMA,
            pltpu.SemaphoreType.DMA((THIRDS,)),
        ],
        compiler_params=pltpu.CompilerParams(vmem_limit_bytes=WIDE_LIMIT),
        cost_estimate=pl.CostEstimate(flops=2 * 2 * occ * capacity * block * width, bytes_accessed=5 << 20, transcendentals=0),
    )(mask, slots, orbitals, packed)


CONTRACT = (((0,), (0,)), ((), ()))


def tile_of(parts, col_refs):
    total, start = None, 0
    for ref in parts:
        rows = ref.shape[0]
        columns = jnp.concatenate([c[start : start + rows, :] for c in col_refs], axis=1)
        term = lax.dot_general(ref[...], columns, CONTRACT, preferred_element_type=jnp.float32)
        total = term if total is None else total + term
        start += rows
    return total


def packed_diagonal(square):
    size = square.shape[0]
    row = lax.broadcasted_iota(jnp.int32, square.shape, 0)
    column = lax.broadcasted_iota(jnp.int32, square.shape, 1)
    left = square - square.astype(jnp.bfloat16).astype(jnp.float32)
    left = jnp.sum(jnp.where(row == column, left, 0.0), axis=0, keepdims=True)
    final = jnp.sum(jnp.where(column[:1] == size - 1, left, 0.0), axis=1, keepdims=True)
    left = jnp.where((row == size - 1) & (column == 0), final, left)
    return jnp.where(row > column, left, square)


def unpacked_diagonal(square):
    size = square.shape[0]
    row = lax.broadcasted_iota(jnp.int32, square.shape, 0)
    column = lax.broadcasted_iota(jnp.int32, square.shape, 1)
    bottom = square[size - 1 :, :]
    final = jnp.sum(jnp.where(column[:1] == 0, bottom, 0.0), axis=1, keepdims=True)
    left = jnp.where(column[:1] == 0, square[size - 2 : size - 1, :], bottom)
    left = jnp.where(column[:1] == size - 1, final, left)
    whole = jnp.where(row > column, square.T, square)
    return jnp.where(row == column, square + left, whole)


def early_kernel(orders, own, *refs):
    count = len(orders)
    col_refs, moved = refs[:4], refs[4 : 4 + count]
    out_refs = refs[4 + count : -2]
    held, sems = refs[-2:]
    copies = [pltpu.make_async_copy(ref, held.at[n], sems.at[n]) for n, ref in enumerate(moved)]
    for copy in copies:
        copy.start()
    filled = [0, 0]
    for n, (group, order) in enumerate(orders):
        copies[n].wait()
        tile = tile_of([held.at[n]], [col_refs[o] for o in order])
        if own and n == 0:
            size = tile.shape[0]
            tile = jnp.concatenate([packed_diagonal(tile[:, :size]), tile[:, size:]], axis=1)
        out_refs[group][filled[group]] = tile.astype(out_refs[group].dtype)
        filled[group] += 1


def early_tiles(col_panels, kept, sent, own):
    depth, width = col_panels[0].shape
    orders = [(0, (0, 1, 2, 3))] * len(kept) + [(1, (1, 0, 3, 2))] * len(sent)
    vmem = pl.BlockSpec(memory_space=pltpu.VMEM)
    return pl.pallas_call(
        functools.partial(early_kernel, orders, own),
        out_shape=tuple(
            jax.ShapeDtypeStruct((len(group), width, 4 * width), jnp.bfloat16) for group in (kept, sent)
        ),
        in_specs=[vmem] * 4 + [pl.BlockSpec(memory_space=pl.ANY)] * len(orders),
        out_specs=(vmem, vmem),
        scratch_shapes=[
            pltpu.VMEM((len(orders), depth, width), jnp.bfloat16),
            pltpu.SemaphoreType.DMA((len(orders),)),
        ],
        compiler_params=pltpu.CompilerParams(vmem_limit_bytes=VMEM_LIMIT),
        cost_estimate=pl.CostEstimate(flops=8 * width * width * depth * len(orders), bytes_accessed=7 << 20, transcendentals=0),
    )(*col_panels, *kept, *sent)


def last_kernel(ring, *refs):
    col_refs, far_ref, out_ref = refs[4:8], refs[8], refs[9]
    near_ref, outer_ref, near_other_ref, outer_other_ref = refs[:4]
    col, core = lax.axis_index("col"), lax.rem(lax.axis_index("row"), 2)

    def origin(d):
        return lax.rem(col + jnp.where(core == 0, d, ring - d), ring)

    for d in range(3):
        out_ref[origin(d)] = near_ref[d]
    out_ref[origin(3)] = outer_ref[0]
    for d in range(1, 3):
        out_ref[origin(ring - d)] = near_other_ref[d - 1]
    out_ref[origin(ring - 3)] = outer_other_ref[0]
    out_ref[origin(4)] = tile_of([far_ref], col_refs).astype(out_ref.dtype)


def last_tile(done, col_panels, far, ring):
    depth, width = far.shape
    return pl.pallas_call(
        functools.partial(last_kernel, ring),
        out_shape=jax.ShapeDtypeStruct((ring, width, 4 * width), jnp.bfloat16),
        in_specs=[pl.BlockSpec(memory_space=pltpu.VMEM)] * 9,
        out_specs=pl.BlockSpec(memory_space=pltpu.VMEM),
        compiler_params=pltpu.CompilerParams(vmem_limit_bytes=VMEM_LIMIT),
        cost_estimate=pl.CostEstimate(flops=8 * width * width * depth, bytes_accessed=6 << 20, transcendentals=0),
    )(*done, *col_panels, far)


def sum_kernel(in_ref, out_ref):
    row = lax.axis_index("row")
    width = out_ref.shape[2]
    for rho in range(out_ref.shape[1]):
        total = None
        for a in range(in_ref.shape[0]):
            term = in_ref[a, :, rho * width : (rho + 1) * width].astype(jnp.float32)
            total = term if total is None else total + term
        out_ref[:, row ^ rho, :] = total
        if rho == 0:
            @pl.when(lax.axis_index("aux") == lax.axis_index("col"))
            def _(total=total):
                out_ref[:, row, :] = unpacked_diagonal(total)


def sum_parts(received):
    count, width, wide = received.shape
    return pl.pallas_call(
        sum_kernel,
        out_shape=jax.ShapeDtypeStruct((width, wide // width, width), jnp.float32),
        in_specs=[pl.BlockSpec(memory_space=pltpu.VMEM)],
        out_specs=pl.BlockSpec(memory_space=pltpu.VMEM),
        compiler_params=pltpu.CompilerParams(vmem_limit_bytes=VMEM_LIMIT),
        cost_estimate=pl.CostEstimate(flops=count * width * wide, bytes_accessed=2 * count * width * wide, transcendentals=0),
    )(received)


def local(integrals, block_mask, block_slots, orbitals):
    ring, rows_n = lax.axis_size("col"), lax.axis_size("row")
    whole = half_transform(block_mask[0], block_slots[0], integrals[0], orbitals)

    along = [
        (r * ring + z, r * ring + (z + (ring - 1 if r % 2 == 0 else 1)) % ring)
        for r in range(rows_n)
        for z in range(ring)
    ]

    def hop(panel):
        return lax.ppermute(panel, ("row", "col"), along)

    def to_row(value, rho):
        return lax.ppermute(value, "row", [(i, i ^ rho) for i in range(rows_n)])

    kept = [whole, hop(whole)]
    beside = to_row(whole, 1)
    over = to_row(whole, 2)
    sent = [hop(beside)]
    kept.append(hop(kept[1]))
    sent.append(hop(sent[0]))
    over, kept[2] = lax.optimization_barrier((over, kept[2]))
    diagonal = to_row(over, 1)
    col_panels = [whole, beside, over, diagonal]
    near = early_tiles(col_panels, kept, sent, True)
    third = hop(kept[2])
    third_sent = hop(sent[1])
    near_kept, near_sent, third = lax.optimization_barrier((*near, third))
    far = hop(third)
    near_other = to_row(near_sent, 1)
    outer_kept, outer_sent = early_tiles(col_panels, [third], [third_sent], False)
    outer_other = to_row(outer_sent, 1)
    sums = last_tile([near_kept, outer_kept, near_other, outer_other], col_panels, far, ring)
    received = lax.all_to_all(sums, "aux", 0, 0, tiled=True)
    return sum_parts(received)


def solution(mesh):
    placed = (
        P("aux", ("row", "col"), None, None),
        P("aux", ("row", "col"), None),
        P("aux", ("row", "col"), None),
        P(),
    )
    return jax.shard_map(
        local, mesh=mesh, in_specs=placed, out_specs=P(("row", "aux"), None, "col"), check_vma=False
    )
```

```python
import functools

import jax
import jax.numpy as jnp
from jax import lax
from jax.experimental import pallas as pl
from jax.experimental.pallas import tpu as pltpu
from jax.sharding import PartitionSpec as P

WIDE_LIMIT = 60 * 1024 * 1024
VMEM_LIMIT = 16 * 1024 * 1024
CHUNKS = 2


def half_kernel(mask_ref, slot_ref, orb_ref, int_ref, whole_ref,
                place_ref, weight_ref, orb_buf, int_buf, out_buf, int_sem, orb_sem, out_sem):
    chunks, capacity, block, lanes = int_buf.shape
    rows = out_buf.shape[1]
    occ = orb_buf.shape[0]
    row_blocks, block_count = mask_ref.shape
    low = lax.broadcasted_iota(jnp.int32, (occ, 2 * block), 1) < block

    def load(c):
        return pltpu.make_async_copy(int_ref.at[:, :, pl.ds(c * lanes, lanes)], int_buf.at[c], int_sem.at[c])

    orb_load = pltpu.make_async_copy(orb_ref, orb_buf, orb_sem)
    orb_load.start()
    for c in range(chunks):
        load(c).start()

    position = lax.broadcasted_iota(jnp.int32, mask_ref.shape, 0) * block_count + lax.broadcasted_iota(
        jnp.int32, mask_ref.shape, 1
    )
    slots = jnp.where(mask_ref[...] == 1, slot_ref[...], -1)
    for s in range(capacity):
        place_ref[s] = jnp.max(jnp.where(slots == s, position, -1))

    orb_load.wait()
    for pair in range(capacity // 2):
        parts = []
        for s in (2 * pair, 2 * pair + 1):
            place = place_ref[s]
            at = jnp.maximum(place, 0)
            home = at // block_count
            parity = lax.rem(at, 2)
            start = pl.multiple_of((lax.rem(at, block_count) // 2) * (2 * block), 2 * block)
            columns = orb_buf[:, pl.ds(start, 2 * block)].astype(jnp.float32)
            turned = pltpu.roll(columns, block, 1)
            value = jnp.where(parity == (s % 2), columns, turned)
            parts.append((place, home, value))
        for b in range(row_blocks):
            chosen = [jnp.where((place >= 0) & (home == b), value, 0.0) for place, home, value in parts]
            weight_ref[b * occ : (b + 1) * occ, pair * 2 * block : (pair + 1) * 2 * block] = jnp.where(
                low, chosen[0], chosen[1]
            ).astype(weight_ref.dtype)

    def store(c):
        return pltpu.make_async_copy(out_buf.at[c], whole_ref.at[pl.ds(c * rows, rows)], out_sem.at[c])

    for c in range(chunks):
        load(c).wait()
        packed = int_buf[c].reshape(capacity * block, lanes)
        product = jnp.dot(weight_ref[...], packed, preferred_element_type=jnp.float32)
        for pair in range(lanes // (2 * block)):
            first = product[:occ, pair * 2 * block : (pair + 1) * 2 * block]
            second = product[occ:, pair * 2 * block : (pair + 1) * 2 * block]
            out_buf[c, 2 * pair * occ : (2 * pair + 1) * occ, :] = jnp.where(
                low, first, pltpu.roll(second, block, 1)
            ).astype(out_buf.dtype)
            out_buf[c, (2 * pair + 1) * occ : (2 * pair + 2) * occ, :] = jnp.where(
                low, pltpu.roll(first, block, 1), second
            ).astype(out_buf.dtype)
        store(c).start()
    for c in range(chunks):
        store(c).wait()


def half_transform(mask, slots, packed, orbitals):
    capacity, block, width = packed.shape
    occ = orbitals.shape[0]
    lanes = width // CHUNKS
    rows = lanes // block * occ
    vmem = pl.BlockSpec(memory_space=pltpu.VMEM)
    anywhere = pl.BlockSpec(memory_space=pl.ANY)
    return pl.pallas_call(
        half_kernel,
        out_shape=jax.ShapeDtypeStruct((rows * CHUNKS, 2 * block), jnp.bfloat16),
        in_specs=[vmem, vmem, anywhere, anywhere],
        out_specs=anywhere,
        scratch_shapes=[
            pltpu.SMEM((capacity,), jnp.int32),
            pltpu.VMEM((2 * occ, capacity * block), jnp.bfloat16),
            pltpu.VMEM(orbitals.shape, jnp.bfloat16),
            pltpu.VMEM((CHUNKS, capacity, block, lanes), jnp.bfloat16),
            pltpu.VMEM((CHUNKS, rows, 2 * block), jnp.bfloat16),
            pltpu.SemaphoreType.DMA((CHUNKS,)),
            pltpu.SemaphoreType.DMA,
            pltpu.SemaphoreType.DMA((CHUNKS,)),
        ],
        compiler_params=pltpu.CompilerParams(vmem_limit_bytes=WIDE_LIMIT),
        cost_estimate=pl.CostEstimate(flops=2 * 2 * occ * capacity * block * width, bytes_accessed=5 << 20, transcendentals=0),
    )(mask, slots, orbitals, packed)


CONTRACT = (((0,), (0,)), ((), ()))


def tile_of(parts, col_refs):
    total, start = None, 0
    for ref in parts:
        rows = ref.shape[0]
        columns = jnp.concatenate([c[start : start + rows, :] for c in col_refs], axis=1)
        term = lax.dot_general(ref[...], columns, CONTRACT, preferred_element_type=jnp.float32)
        total = term if total is None else total + term
        start += rows
    return total


def packed_diagonal(square):
    size = square.shape[0]
    row = lax.broadcasted_iota(jnp.int32, square.shape, 0)
    column = lax.broadcasted_iota(jnp.int32, square.shape, 1)
    left = square - square.astype(jnp.bfloat16).astype(jnp.float32)
    left = jnp.sum(jnp.where(row == column, left, 0.0), axis=0, keepdims=True)
    final = jnp.sum(jnp.where(column[:1] == size - 1, left, 0.0), axis=1, keepdims=True)
    left = jnp.where((row == size - 1) & (column == 0), final, left)
    return jnp.where(row > column, left, square)


def unpacked_diagonal(square):
    size = square.shape[0]
    row = lax.broadcasted_iota(jnp.int32, square.shape, 0)
    column = lax.broadcasted_iota(jnp.int32, square.shape, 1)
    bottom = square[size - 1 :, :]
    final = jnp.sum(jnp.where(column[:1] == 0, bottom, 0.0), axis=1, keepdims=True)
    left = jnp.where(column[:1] == 0, square[size - 2 : size - 1, :], bottom)
    left = jnp.where(column[:1] == size - 1, final, left)
    whole = jnp.where(row > column, square.T, square)
    return jnp.where(row == column, square + left, whole)


def early_kernel(orders, own, *refs):
    count = len(orders)
    col_refs, moved = refs[:4], refs[4 : 4 + count]
    out_refs = refs[4 + count : -2]
    held, sems = refs[-2:]
    copies = [pltpu.make_async_copy(ref, held.at[n], sems.at[n]) for n, ref in enumerate(moved)]
    for copy in copies:
        copy.start()
    filled = [0, 0]
    for n, (group, order) in enumerate(orders):
        copies[n].wait()
        tile = tile_of([held.at[n]], [col_refs[o] for o in order])
        if own and n == 0:
            size = tile.shape[0]
            tile = jnp.concatenate([packed_diagonal(tile[:, :size]), tile[:, size:]], axis=1)
        out_refs[group][filled[group]] = tile.astype(out_refs[group].dtype)
        filled[group] += 1


def early_tiles(col_panels, kept, sent, own):
    depth, width = col_panels[0].shape
    orders = [(0, (0, 1, 2, 3))] * len(kept) + [(1, (1, 0, 3, 2))] * len(sent)
    vmem = pl.BlockSpec(memory_space=pltpu.VMEM)
    return pl.pallas_call(
        functools.partial(early_kernel, orders, own),
        out_shape=tuple(
            jax.ShapeDtypeStruct((len(group), width, 4 * width), jnp.bfloat16) for group in (kept, sent)
        ),
        in_specs=[vmem] * 4 + [pl.BlockSpec(memory_space=pl.ANY)] * len(orders),
        out_specs=(vmem, vmem),
        scratch_shapes=[
            pltpu.VMEM((len(orders), depth, width), jnp.bfloat16),
            pltpu.SemaphoreType.DMA((len(orders),)),
        ],
        compiler_params=pltpu.CompilerParams(vmem_limit_bytes=VMEM_LIMIT),
        cost_estimate=pl.CostEstimate(flops=8 * width * width * depth * len(orders), bytes_accessed=7 << 20, transcendentals=0),
    )(*col_panels, *kept, *sent)


def last_kernel(ring, *refs):
    col_refs, far_ref, out_ref = refs[4:8], refs[8], refs[9]
    near_ref, outer_ref, near_other_ref, outer_other_ref = refs[:4]
    col, core = lax.axis_index("col"), lax.rem(lax.axis_index("row"), 2)

    def origin(d):
        return lax.rem(col + jnp.where(core == 0, d, ring - d), ring)

    for d in range(3):
        out_ref[origin(d)] = near_ref[d]
    out_ref[origin(3)] = outer_ref[0]
    for d in range(1, 3):
        out_ref[origin(ring - d)] = near_other_ref[d - 1]
    out_ref[origin(ring - 3)] = outer_other_ref[0]
    out_ref[origin(4)] = tile_of([far_ref], col_refs).astype(out_ref.dtype)


def last_tile(done, col_panels, far, ring):
    depth, width = far.shape
    return pl.pallas_call(
        functools.partial(last_kernel, ring),
        out_shape=jax.ShapeDtypeStruct((ring, width, 4 * width), jnp.bfloat16),
        in_specs=[pl.BlockSpec(memory_space=pltpu.VMEM)] * 9,
        out_specs=pl.BlockSpec(memory_space=pltpu.VMEM),
        compiler_params=pltpu.CompilerParams(vmem_limit_bytes=VMEM_LIMIT),
        cost_estimate=pl.CostEstimate(flops=8 * width * width * depth, bytes_accessed=6 << 20, transcendentals=0),
    )(*done, *col_panels, far)


def sum_kernel(in_ref, out_ref):
    row = lax.axis_index("row")
    width = out_ref.shape[2]
    for rho in range(out_ref.shape[1]):
        total = None
        for a in range(in_ref.shape[0]):
            term = in_ref[a, :, rho * width : (rho + 1) * width].astype(jnp.float32)
            total = term if total is None else total + term
        out_ref[:, row ^ rho, :] = total
        if rho == 0:
            @pl.when(lax.axis_index("aux") == lax.axis_index("col"))
            def _(total=total):
                out_ref[:, row, :] = unpacked_diagonal(total)


def sum_parts(received):
    count, width, wide = received.shape
    return pl.pallas_call(
        sum_kernel,
        out_shape=jax.ShapeDtypeStruct((width, wide // width, width), jnp.float32),
        in_specs=[pl.BlockSpec(memory_space=pltpu.VMEM)],
        out_specs=pl.BlockSpec(memory_space=pltpu.VMEM),
        compiler_params=pltpu.CompilerParams(vmem_limit_bytes=VMEM_LIMIT),
        cost_estimate=pl.CostEstimate(flops=count * width * wide, bytes_accessed=2 * count * width * wide, transcendentals=0),
    )(received)


def local(integrals, block_mask, block_slots, orbitals):
    ring, rows_n = lax.axis_size("col"), lax.axis_size("row")
    whole = half_transform(block_mask[0], block_slots[0], integrals[0], orbitals)

    along = [
        (r * ring + z, r * ring + (z + (ring - 1 if r % 2 == 0 else 1)) % ring)
        for r in range(rows_n)
        for z in range(ring)
    ]

    def hop(panel):
        return lax.ppermute(panel, ("row", "col"), along)

    def to_row(value, rho):
        return lax.ppermute(value, "row", [(i, i ^ rho) for i in range(rows_n)])

    kept = [whole, hop(whole)]
    beside = to_row(whole, 1)
    over = to_row(whole, 2)
    sent = [hop(beside)]
    kept.append(hop(kept[1]))
    sent.append(hop(sent[0]))
    over, kept[2] = lax.optimization_barrier((over, kept[2]))
    diagonal = to_row(over, 1)
    col_panels = [whole, beside, over, diagonal]
    near = early_tiles(col_panels, kept, sent, True)
    third = hop(kept[2])
    third_sent = hop(sent[1])
    near_kept, near_sent = near
    far = hop(third)
    near_other = to_row(near_sent, 1)
    outer_kept, outer_sent = early_tiles(col_panels, [third], [third_sent], False)
    outer_other = to_row(outer_sent, 1)
    sums = last_tile([near_kept, outer_kept, near_other, outer_other], col_panels, far, ring)
    received = lax.all_to_all(sums, "aux", 0, 0, tiled=True)
    return sum_parts(received)


def solution(mesh):
    placed = (
        P("aux", ("row", "col"), None, None),
        P("aux", ("row", "col"), None),
        P("aux", ("row", "col"), None),
        P(),
    )
    return jax.shard_map(
        local, mesh=mesh, in_specs=placed, out_specs=P(("row", "aux"), None, "col"), check_vma=False
    )
```
